128 devices in a mesh: owner: 8 (over x, core), fsdp: 16 (over y, z).
Axes of the slice: x: 4, y: 4, z: 4, core: 2. Of those that a mesh axis runs over, the one named last changes fastest.
Arguments:
- precond: bfloat16 [8, 2048, 2048], P('owner', 'fsdp'), as said below
- basis_old: bfloat16 [8, 2048, 2048], P('owner', 'fsdp'), as said below
- gradient: bfloat16 [16384, 8192], P('owner', 'fsdp'), may hold values from -6 to 6
- moment_in: float32 [16384, 8192], P('owner', 'fsdp')
- second_in: float32 [16384, 8192], P('owner', 'fsdp'), may hold values from 0.3 to 3
Outputs:
- update: bfloat16 [16384, 8192], P('owner', 'fsdp')
- moment_one: float32 [16384, 8192], P('owner', 'fsdp')
- moment_two: float32 [16384, 8192], P('owner', 'fsdp')
- basis_new: float32 [8, 2048, 2048], P('owner', 'fsdp')
The draws below stay inside these ranges and needn't reach their ends.
Inputs may be any that keep to these rules, and one draw needn't show every extreme that they name: Each block of precond is symmetric and positive definite. Each block of basis_old is invertible.
All inputs are finite; a program needn't handle non-finite values.
Results may differ from the reference program's by a relative error of at most 0.024.
Values may be sent and summed in bfloat16 or wider, within the bound.
No kernel may reach another device: no remote copies, remote signals or barrier semaphores. Data moves between devices by JAX's collectives and lax.ppermute only.
A program may use at most 192 MiB of HBM per device.

```python
import math
import jax
import jax.numpy as jnp
from jax import lax

D = 8192
B = 2048
NBLK = 8
ROWS = 16384


def draw_precond(key, part):
    key = jax.random.fold_in(key, 11)
    first, second, third = jax.random.split(key, 3)
    noise = jax.random.normal(first, (NBLK, B, B), jnp.float32)
    symmetric = (noise + jnp.swapaxes(noise, 1, 2)) * (1.0 / jnp.sqrt(2.0 * B))
    diagonal = jnp.exp(jax.random.uniform(second, (NBLK, B), jnp.float32, jnp.log(3.0), jnp.log(6.0)))
    direction = jnp.abs(jax.random.normal(third, (NBLK, B), jnp.float32)) * (1.0 / jnp.sqrt(1.0 * B))
    spike = 20.0 * direction[:, :, None] * direction[:, None, :]
    eye_full = jnp.eye(B, dtype=jnp.float32)
    return (symmetric + spike + eye_full[None, :, :] * diagonal[:, :, None]).astype(jnp.bfloat16)


def draw_basis_old(key, part):
    key = jax.random.fold_in(key, 23)
    noise = jax.random.normal(key, (NBLK, B, B), jnp.float32)
    eye_full = jnp.eye(B, dtype=jnp.float32)
    return (eye_full[None, :, :] + 0.3 * noise / jnp.sqrt(1.0 * B)).astype(jnp.bfloat16)


def draw_moment_in(key, part):
    key = jax.random.fold_in(key, 37)
    first, second, third = jax.random.split(key, 3)
    row_pos = jnp.arange(ROWS, dtype=jnp.float32) / max(ROWS - 1, 1)
    col_pos = jnp.arange(D, dtype=jnp.float32) / max(D - 1, 1)
    rough_rows = jnp.exp(jax.random.uniform(second, (ROWS, 1), jnp.float32, -0.25, 0.25))
    rough_cols = jnp.exp(jax.random.uniform(third, (1, D), jnp.float32, -0.25, 0.25))
    row_ramp = 3.0 ** row_pos
    col_ramp = 3.0 ** col_pos
    noise = jax.random.normal(first, (ROWS, D), jnp.float32)
    values = 0.3 * row_ramp[:, None] * col_ramp[None, :] * rough_rows * rough_cols * noise
    return values.astype(jnp.float32)


def block_levels(rng, extent, pieces, smallest, high):
    def one(position, shards_of):
        heights = jax.random.uniform(jax.random.fold_in(jax.random.fold_in(rng, 6), position), (shards_of,), jnp.float32, smallest / len(pieces), high / len(pieces))
        return jnp.repeat(jnp.exp(heights), extent[position] // shards_of).reshape((-1,) + (1,) * (len(extent) - position - 1))

    level = one(*pieces[0])
    for cut in pieces[1:]:
        level = level * one(*cut)
    return level


def centred(stream_key, dims, spread, reach, cuts=(), kind=jnp.bfloat16):
    drawn = jax.random.normal(stream_key, dims, jnp.float32) * spread
    if len(cuts) > 0:
        drawn = block_levels(stream_key, dims, cuts, -0.22, 0.18) * drawn
    return jnp.clip(drawn, min=-reach, max=reach).astype(kind)


def setup_inputs(seed: int = 0) -> dict:
    key_list = jax.random.split(jax.random.key(seed), 6)
    precond = draw_precond(jax.random.fold_in(key_list[5], 71), 0)
    basis_old = draw_basis_old(jax.random.fold_in(key_list[5], 71), 0)
    gradient = centred(key_list[2], (ROWS, D), 1.0, 6.0, ((0, 8), (1, 16)))
    moment_in = draw_moment_in(jax.random.fold_in(key_list[5], 71), 0)
    second_in = jnp.clip(jnp.exp(math.log(3.0) - 2.3025851 * jax.random.uniform(key_list[4], (ROWS, D), jnp.float32) ** block_levels(key_list[4], (ROWS, D), ((0, 8), (1, 16)), -0.2, 0.2)), 0.3, 3.0)
    return dict(precond=precond, basis_old=basis_old, gradient=gradient, moment_in=moment_in, second_in=second_in)


beta_one = 0.9
beta_two = 0.95
small_eps = 1e-08
norm_eps = 1e-06

def orthonormal(chol, power):

    def solve_one(factor, rows):
        return jax.scipy.linalg.solve_triangular(factor, rows.T, lower=True).T
    return jax.vmap(solve_one)(chol, power)

def reference(precond, basis_old, gradient, moment_in, second_in):
    upper_limit = lax.Precision.HIGHEST
    power = jnp.einsum('bik,bkj->bij', precond.astype(jnp.float32), basis_old.astype(jnp.float32), precision=upper_limit)
    power_half = lax.optimization_barrier(power.astype(jnp.bfloat16))
    power_wide = power_half.astype(jnp.float32)
    gram_sum = jnp.einsum('bki,bkj->bij', power_wide, power_wide, precision=upper_limit)
    chol = jnp.linalg.cholesky(gram_sum)
    basis_new = orthonormal(chol, power_wide)
    basis_half = basis_new.astype(jnp.bfloat16)
    moment_one = beta_one * moment_in + (1.0 - beta_one) * gradient.astype(jnp.float32)
    moment_half = moment_one.astype(jnp.bfloat16)
    broad_basis_matrix = basis_half.astype(jnp.float32)
    gradient_block_list = gradient.reshape(NBLK, B, D).astype(jnp.float32)
    moment_block_list = moment_half.reshape(NBLK, B, D).astype(jnp.float32)
    rotated_gradient = jnp.einsum('aos,aol->asl', broad_basis_matrix, gradient_block_list, precision=upper_limit)
    rotated_moment = jnp.einsum('aos,aol->asl', broad_basis_matrix, moment_block_list, precision=upper_limit)
    moment_two = beta_two * second_in + (1.0 - beta_two) * jnp.square(rotated_gradient.reshape(ROWS, D))
    step_ratio = (rotated_moment / (jnp.sqrt(moment_two.reshape(NBLK, B, D)) + small_eps)).astype(jnp.bfloat16)
    unscaled_update = jnp.einsum('rfu,rup->rfp', broad_basis_matrix, step_ratio.astype(jnp.float32), precision=upper_limit)
    total = jnp.sum(unscaled_update * unscaled_update)
    scale = jnp.sqrt(jnp.float32(ROWS * D)) / (jnp.sqrt(total) + norm_eps)
    update = (unscaled_update * scale).reshape(ROWS, D).astype(jnp.bfloat16)
    return (update, moment_one, moment_two, basis_new)
```

```python
import functools
import jax
import jax.numpy as jnp
from jax import lax
from jax.experimental import pallas as pl
from jax.experimental.pallas import tpu as pltpu
from jax.sharding import PartitionSpec as P

beta_one = 0.9
beta_two = 0.95
small_eps = 1e-08
norm_eps = 1e-06
NN = (((1,), (0,)), ((), ()))
NT = (((1,), (1,)), ((), ()))
TN = (((0,), (0,)), ((), ()))
CH = 256
FIRST = 512

def lane_splat(row, lane):
    return jnp.broadcast_to(row[:, lane:lane+1], (8, 128))

def diag_pick(row, start):
    idx = lax.broadcasted_iota(jnp.int32, (8, 128), 0) + start
    return jnp.take_along_axis(row, idx, axis=1, mode="promise_in_bounds")

def invert_factor(A):
    sub = lax.broadcasted_iota(jnp.int32, (8, 128), 0)
    lane = lax.broadcasted_iota(jnp.int32, (8, 128), 1)
    A = list(A)
    X = [(lane == sub + 8 * g).astype(jnp.float32) for g in range(16)]
    for g in range(16):
        r = [jnp.broadcast_to(A[g][k:k+1, :], (8, 128)) for k in range(8)]
        x = [jnp.broadcast_to(X[g][k:k+1, :], (8, 128)) for k in range(8)]
        d = {}
        for j in range(8):
            for i in range(j, 8):
                d[i, j] = lane_splat(r[j], 8 * g + i)
        for k in range(8):
            rs = lax.rsqrt(d[k, k])
            rd = rs * rs
            for i in range(k + 1, 8):
                m = d[i, k] * rd
                for j in range(k + 1, i + 1):
                    d[i, j] = d[i, j] - m * d[j, k]
                r[i] = r[i] - m * r[k]
                x[i] = x[i] - m * x[k]
            r[k] = r[k] * rs
            x[k] = x[k] * rs
        for h in range(g + 1, 16):
            for k in range(8):
                l = diag_pick(r[k], 8 * h)
                A[h] = A[h] - l * r[k]
                X[h] = X[h] - l * x[k]
        z = x[0]
        for k in range(1, 8):
            z = jnp.where(sub == k, x[k], z)
        X[g] = z
    return X


def mm(a, b, dims=NN):
    return lax.dot_general(a, b, dims, preferred_element_type=jnp.float32)

def split(x):
    high = x.astype(jnp.bfloat16)
    return high, (x - high.astype(jnp.float32)).astype(jnp.bfloat16)

def mm3(a, b, dims=NN):
    ah, al = split(a)
    bh, bl = split(b)
    return mm(ah, bh, dims) + (mm(al, bh, dims) + mm(ah, bl, dims))

def inverse_of_rows(block):
    rows = invert_factor([block[8 * i:8 * i + 8, :] for i in range(16)])
    return jnp.concatenate(rows, axis=0)

def kernel(prev, count, *refs):
    if prev:
        t_ref, ph_ref, pl_ref, rh, rl, v = refs
        rh[0:prev, :] = ph_ref[...]
        rl[0:prev, :] = pl_ref[...]
    else:
        t_ref, rh, rl, v = refs

    def chunk(ci, carry):
        row = pl.multiple_of(ci * CH, CH)
        out = pl.multiple_of(prev + ci * CH, CH)
        t = t_ref[pl.ds(row, CH), :]
        v[...] = t.astype(jnp.float32)

        def remove(p, carry):
            at = pl.ds(pl.multiple_of(p * CH, CH), CH)
            qh = rh[at, :]
            ql = rl[at, :]
            t = t_ref[pl.ds(row, CH), :]
            s = mm(t, qh, NT) + mm(t, ql, NT)
            sh, sl = split(s)
            v[...] -= mm(sh, qh) + (mm(sl, qh) + mm(sh, ql))
            return carry

        lax.fori_loop(0, prev // CH + ci, remove, 0)
        vh, vl = split(v[...])
        g = mm(vh, vh, NT) + (mm(vh, vl, NT) + mm(vl, vh, NT))
        h = CH // 2
        x1 = inverse_of_rows(g[:h, :h])
        u = mm3(x1, g[:h, h:])
        ut = u.T
        s = g[h:, h:] - mm3(ut, u)
        w = mm3(ut, x1)
        x2 = inverse_of_rows(s)
        x21 = -mm3(x2, w)
        x = jnp.concatenate([jnp.concatenate([x1, jnp.zeros((h, h), jnp.float32)], axis=1),
                             jnp.concatenate([x21, x2], axis=1)], axis=0)
        xh, xl = split(x)
        vh, vl = split(v[...])
        q = mm(xh, vh) + (mm(xl, vh) + mm(xh, vl))
        qh, ql = split(q)
        rh[pl.ds(out, CH), :] = qh
        rl[pl.ds(out, CH), :] = ql
        return carry

    lax.fori_loop(0, count // CH, chunk, 0)

def orthogonal_rows(t, done=None):
    count, width = t.shape
    prev = 0 if done is None else done[0].shape[0]
    shape = jax.ShapeDtypeStruct((prev + count, width), jnp.bfloat16)
    args = (t,) if done is None else (t,) + tuple(done)
    n = prev + count
    return pl.pallas_call(
        functools.partial(kernel, prev, count),
        out_shape=(shape, shape),
        scratch_shapes=[pltpu.VMEM((CH, width), jnp.float32)],
        compiler_params=pltpu.CompilerParams(vmem_limit_bytes=56 * 1024 * 1024),
    )(*args)


def sum_over_all(x):
    for axis in ("owner", "fsdp"):
        size = lax.axis_size(axis)
        step = 1
        while step < size:
            x = x + lax.ppermute(x, axis, [(i, i ^ step) for i in range(size)])
            step *= 2
    return x


def on_device(precond, basis_old, gradient, moment_in, second_in):
    order = precond.shape[2]
    width = gradient.shape[1]
    both = jnp.concatenate([precond[0], basis_old[0, :, :FIRST]], axis=1)
    both = lax.all_gather(both, "fsdp", axis=0, tiled=True)
    factor = both[:, :order]
    later = lax.all_gather(basis_old[0, :, FIRST:], "fsdp", axis=0, tiled=True)
    moment_one = beta_one * moment_in + (1.0 - beta_one) * gradient.astype(jnp.float32)
    moment_half = moment_one.astype(jnp.bfloat16)
    first_rows = mm(both[:, order:], factor, TN).astype(jnp.bfloat16)
    first = orthogonal_rows(first_rows)
    later_rows = mm(later, factor, TN).astype(jnp.bfloat16)
    high, low = orthogonal_rows(later_rows, first)
    part = order // lax.axis_size("fsdp")
    start = lax.axis_index("fsdp") * part
    basis_new = (
        lax.dynamic_slice_in_dim(high, start, part, 1).astype(jnp.float32)
        + lax.dynamic_slice_in_dim(low, start, part, 1).astype(jnp.float32)
    ).T[None]
    rotated_gradient = mm(high, gradient)
    rotated_moment = mm(high, moment_half)
    moment_two = beta_two * second_in + (1.0 - beta_two) * jnp.square(rotated_gradient)
    step_ratio = (rotated_moment / (jnp.sqrt(moment_two) + small_eps)).astype(jnp.bfloat16)
    unscaled_update = mm(high, step_ratio, TN)
    total = sum_over_all(jnp.sum(unscaled_update * unscaled_update).reshape(1, 1))
    count = gradient.shape[0] * lax.axis_size("owner") * width * lax.axis_size("fsdp")
    scale = jnp.sqrt(jnp.float32(count)) / (jnp.sqrt(total) + norm_eps)
    update = (unscaled_update * scale).astype(jnp.bfloat16)
    return (update, moment_one, moment_two, basis_new)


def solution(mesh):
    return jax.shard_map(
        on_device,
        mesh=mesh,
        in_specs=(
            P("owner", "fsdp", None),
            P("owner", "fsdp", None),
            P("owner", "fsdp"),
            P("owner", "fsdp"),
            P("owner", "fsdp"),
        ),
        out_specs=(
            P("owner", "fsdp"),
            P("owner", "fsdp"),
            P("owner", "fsdp"),
            P("owner", "fsdp", None),
        ),
        check_vma=False,
    )
```

```python
import functools
import jax
import jax.numpy as jnp
from jax import lax
from jax.experimental import pallas as pl
from jax.experimental.pallas import tpu as pltpu
from jax.sharding import PartitionSpec as P

beta_one = 0.9
beta_two = 0.95
small_eps = 1e-08
norm_eps = 1e-06
NN = (((1,), (0,)), ((), ()))
NT = (((1,), (1,)), ((), ()))
TN = (((0,), (0,)), ((), ()))
CH = 256
FIRST = 768

def lane_splat(row, lane):
    return jnp.broadcast_to(row[:, lane:lane+1], (8, 128))

def diag_pick(row, start):
    idx = lax.broadcasted_iota(jnp.int32, (8, 128), 0) + start
    return jnp.take_along_axis(row, idx, axis=1, mode="promise_in_bounds")

def invert_factor(A):
    sub = lax.broadcasted_iota(jnp.int32, (8, 128), 0)
    lane = lax.broadcasted_iota(jnp.int32, (8, 128), 1)
    A = list(A)
    X = [(lane == sub + 8 * g).astype(jnp.float32) for g in range(16)]
    for g in range(16):
        r = [jnp.broadcast_to(A[g][k:k+1, :], (8, 128)) for k in range(8)]
        x = [jnp.broadcast_to(X[g][k:k+1, :], (8, 128)) for k in range(8)]
        d = {}
        for j in range(8):
            for i in range(j, 8):
                d[i, j] = lane_splat(r[j], 8 * g + i)
        for k in range(8):
            rs = lax.rsqrt(d[k, k])
            rd = rs * rs
            for i in range(k + 1, 8):
                m = d[i, k] * rd
                for j in range(k + 1, i + 1):
                    d[i, j] = d[i, j] - m * d[j, k]
                r[i] = r[i] - m * r[k]
                x[i] = x[i] - m * x[k]
            r[k] = r[k] * rs
            x[k] = x[k] * rs
        for h in range(g + 1, 16):
            for k in range(8):
                l = diag_pick(r[k], 8 * h)
                A[h] = A[h] - l * r[k]
                X[h] = X[h] - l * x[k]
        z = x[0]
        for k in range(1, 8):
            z = jnp.where(sub == k, x[k], z)
        X[g] = z
    return X


def mm(a, b, dims=NN):
    return lax.dot_general(a, b, dims, preferred_element_type=jnp.float32)

def split(x):
    high = x.astype(jnp.bfloat16)
    return high, (x - high.astype(jnp.float32)).astype(jnp.bfloat16)

def mm3(a, b, dims=NN):
    ah, al = split(a)
    bh, bl = split(b)
    return mm(ah, bh, dims) + (mm(al, bh, dims) + mm(ah, bl, dims))

def inverse_of_rows(block):
    rows = invert_factor([block[8 * i:8 * i + 8, :] for i in range(16)])
    return jnp.concatenate(rows, axis=0)

def inverse_of_chunk(g):
    h = CH // 2
    x1 = inverse_of_rows(g[:h, :h])
    u = mm3(x1, g[:h, h:])
    ut = u.T
    w = mm3(ut, x1)
    x2 = inverse_of_rows(g[h:, h:] - mm3(ut, u))
    x21 = -mm3(x2, w)
    top = jnp.concatenate([x1, jnp.zeros((h, h), jnp.float32)], axis=1)
    return jnp.concatenate([top, jnp.concatenate([x21, x2], axis=1)], axis=0)

def kernel(prev, count, *refs):
    if prev:
        t_ref, ph_ref, pl_ref, rh, rl, v, vh, vl, sh, sl = refs
        rh[0:prev, :] = ph_ref[...]
        rl[0:prev, :] = pl_ref[...]
    else:
        t_ref, rh, rl, v, vh, vl, sh, sl = refs
    width = t_ref.shape[1]
    tiles = [slice(a, a + CH) for a in range(0, width, CH)]
    chunks = count // CH

    def remove(c, depth):
        slot = c % 2
        t = t_ref[c * CH:(c + 1) * CH, :]
        for p in range(0, depth, CH):
            at = slice(p, p + CH)
            sh[:, at], sl[:, at] = split(mm(t, rh[at, :], NT) + mm(t, rl[at, :], NT))
        for a in tiles:
            x = t_ref[c * CH:(c + 1) * CH, a].astype(jnp.float32)
            if depth:
                x = x - (mm(sh[:, :depth], rh[:depth, a]) + (mm(sl[:, :depth], rh[:depth, a]) + mm(sh[:, :depth], rl[:depth, a])))
            v[slot, :, a] = x
            vh[slot, :, a], vl[slot, :, a] = split(x)

    def products(c, d):
        a, b = c % 2, d % 2
        low = mm(vh[a], vl[b], NT)
        other = low.T if c == d else mm(vl[a], vh[b], NT)
        return mm(vh[a], vh[b], NT) + (low + other)

    def finish(c, x):
        slot = c % 2
        xh, xl = split(x)
        at = slice(prev + c * CH, prev + (c + 1) * CH)
        for a in tiles:
            q = mm(xh, vh[slot, :, a]) + (mm(xl, vh[slot, :, a]) + mm(xh, vl[slot, :, a]))
            rh[at, a], rl[at, a] = split(q)

    def correct(c, s):
        slot = c % 2
        th, tl = split(s.T)
        at = slice(prev + (c - 1) * CH, prev + c * CH)
        for a in tiles:
            x = v[slot, :, a] - (mm(th, rh[at, a]) + (mm(tl, rh[at, a]) + mm(th, rl[at, a])))
            v[slot, :, a] = x
            vh[slot, :, a], vl[slot, :, a] = split(x)

    remove(0, prev)
    g = products(0, 0)
    x = s = None
    for c in range(chunks):
        if c:
            finish(c - 1, x)
            correct(c, s)
        if c + 1 < chunks:
            remove(c + 1, prev + c * CH)
            cross = products(c, c + 1)
            ahead = products(c + 1, c + 1)
        x = inverse_of_chunk(g)
        if c + 1 < chunks:
            s = mm3(x, cross)
            g = ahead - mm3(s.T, s)
    finish(chunks - 1, x)

def orthogonal_rows(t, done=None):
    count, width = t.shape
    prev = 0 if done is None else done[0].shape[0]
    shape = jax.ShapeDtypeStruct((prev + count, width), jnp.bfloat16)
    args = (t,) if done is None else (t,) + tuple(done)
    n = prev + count
    return pl.pallas_call(
        functools.partial(kernel, prev, count),
        out_shape=(shape, shape),
        scratch_shapes=[pltpu.VMEM((2, CH, width), jnp.float32)] + [pltpu.VMEM((2, CH, width), jnp.bfloat16)] * 2
        + [pltpu.VMEM((CH, n), jnp.bfloat16)] * 2,
        compiler_params=pltpu.CompilerParams(vmem_limit_bytes=56 * 1024 * 1024),
    )(*args)


def sum_over_all(x):
    axes = ("owner", "fsdp")
    size = lax.axis_size(axes)
    copies = jnp.broadcast_to(x, (size, 128))
    return jnp.sum(lax.all_to_all(copies, axes, 0, 0, tiled=True)[:, :1], axis=0, keepdims=True)


def on_device(precond, basis_old, gradient, moment_in, second_in):
    order = precond.shape[2]
    width = gradient.shape[1]
    both = jnp.concatenate([precond[0], basis_old[0, :, :FIRST]], axis=1)
    both = lax.all_gather(both, "fsdp", axis=0, tiled=True)
    factor = both[:, :order]
    later = lax.all_gather(basis_old[0, :, FIRST:], "fsdp", axis=0, tiled=True)
    moment_one = beta_one * moment_in + (1.0 - beta_one) * gradient.astype(jnp.float32)
    moment_half = moment_one.astype(jnp.bfloat16)
    first_rows = mm(both[:, order:], factor, TN).astype(jnp.bfloat16)
    first = orthogonal_rows(first_rows)
    later_rows = mm(later, factor, TN).astype(jnp.bfloat16)
    high, low = orthogonal_rows(later_rows, first)
    part = order // lax.axis_size("fsdp")
    start = lax.axis_index("fsdp") * part
    basis_new = (
        lax.dynamic_slice_in_dim(high, start, part, 1).astype(jnp.float32)
        + lax.dynamic_slice_in_dim(low, start, part, 1).astype(jnp.float32)
    ).T[None]
    rotated_gradient = mm(high, gradient)
    rotated_moment = mm(high, moment_half)
    moment_two = beta_two * second_in + (1.0 - beta_two) * jnp.square(rotated_gradient)
    step_ratio = (rotated_moment / (jnp.sqrt(moment_two) + small_eps)).astype(jnp.bfloat16)
    unscaled_update = mm(high, step_ratio, TN)
    total = sum_over_all(jnp.sum(unscaled_update * unscaled_update).reshape(1, 1))
    count = gradient.shape[0] * lax.axis_size("owner") * width * lax.axis_size("fsdp")
    scale = jnp.sqrt(jnp.float32(count)) / (jnp.sqrt(total) + norm_eps)
    update = (unscaled_update * scale).astype(jnp.bfloat16)
    return (update, moment_one, moment_two, basis_new)


def solution(mesh):
    return jax.shard_map(
        on_device,
        mesh=mesh,
        in_specs=(
            P("owner", "fsdp", None),
            P("owner", "fsdp", None),
            P("owner", "fsdp"),
            P("owner", "fsdp"),
            P("owner", "fsdp"),
        ),
        out_specs=(
            P("owner", "fsdp"),
            P("owner", "fsdp"),
            P("owner", "fsdp"),
            P("owner", "fsdp", None),
        ),
        check_vma=False,
    )
```

```python
import functools
import jax
import jax.numpy as jnp
from jax import lax
from jax.experimental import pallas as pl
from jax.experimental.pallas import tpu as pltpu
from jax.sharding import PartitionSpec as P

beta_one = 0.9
beta_two = 0.95
small_eps = 1e-08
norm_eps = 1e-06
NN = (((1,), (0,)), ((), ()))
NT = (((1,), (1,)), ((), ()))
TN = (((0,), (0,)), ((), ()))
CH = 256
FIRST = 1024
BAND = 512

def lane_splat(row, lane):
    return jnp.broadcast_to(row[:, lane:lane+1], (8, 128))

def diag_pick(row, start):
    idx = lax.broadcasted_iota(jnp.int32, (8, 128), 0) + start
    return jnp.take_along_axis(row, idx, axis=1, mode="promise_in_bounds")

def invert_factor(A):
    sub = lax.broadcasted_iota(jnp.int32, (8, 128), 0)
    lane = lax.broadcasted_iota(jnp.int32, (8, 128), 1)
    A = list(A)
    X = [(lane == sub + 8 * g).astype(jnp.float32) for g in range(16)]
    for g in range(16):
        r = [jnp.broadcast_to(A[g][k:k+1, :], (8, 128)) for k in range(8)]
        x = [jnp.broadcast_to(X[g][k:k+1, :], (8, 128)) for k in range(8)]
        d = {}
        for j in range(8):
            for i in range(j, 8):
                d[i, j] = lane_splat(r[j], 8 * g + i)
        for k in range(8):
            rs = lax.rsqrt(d[k, k])
            rd = rs * rs
            for i in range(k + 1, 8):
                m = d[i, k] * rd
                for j in range(k + 1, i + 1):
                    d[i, j] = d[i, j] - m * d[j, k]
                r[i] = r[i] - m * r[k]
                x[i] = x[i] - m * x[k]
            r[k] = r[k] * rs
            x[k] = x[k] * rs
        for h in range(g + 1, 16):
            for k in range(8):
                l = diag_pick(r[k], 8 * h)
                A[h] = A[h] - l * r[k]
                X[h] = X[h] - l * x[k]
        z = x[0]
        for k in range(1, 8):
            z = jnp.where(sub == k, x[k], z)
        X[g] = z
    return X


def mm(a, b, dims=NN):
    return lax.dot_general(a, b, dims, preferred_element_type=jnp.float32)

def split(x):
    high = x.astype(jnp.bfloat16)
    return high, (x - high.astype(jnp.float32)).astype(jnp.bfloat16)

def mm3(a, b, dims=NN):
    ah, al = split(a)
    bh, bl = split(b)
    return mm(ah, bh, dims) + (mm(al, bh, dims) + mm(ah, bl, dims))

def inverse_of_rows(block):
    rows = invert_factor([block[8 * i:8 * i + 8, :] for i in range(16)])
    return jnp.concatenate(rows, axis=0)

def inverse_of_chunk(g):
    h = CH // 2
    x1 = inverse_of_rows(g[:h, :h])
    u = mm3(x1, g[:h, h:])
    ut = u.T
    w = mm3(ut, x1)
    x2 = inverse_of_rows(g[h:, h:] - mm3(ut, u))
    x21 = -mm3(x2, w)
    top = jnp.concatenate([x1, jnp.zeros((h, h), jnp.float32)], axis=1)
    return jnp.concatenate([top, jnp.concatenate([x21, x2], axis=1)], axis=0)

def kernel(prev, count, *refs):
    if prev:
        t_ref, ph_ref, pl_ref, rh, own, v, vh, vl, sh, sl, rl = refs
        rh[0:prev, :] = ph_ref[...]
        rl[0:prev, :] = pl_ref[...]
    else:
        t_ref, rh, rl, v, vh, vl, sh, sl = refs
    width = t_ref.shape[1]
    tiles = [slice(a, a + CH) for a in range(0, width, CH)]
    chunks = count // CH

    def remove(c, depth):
        slot = c % 2
        t = t_ref[c * CH:(c + 1) * CH, :]
        for p in range(0, depth, CH):
            at = slice(p, p + CH)
            sh[:, at], sl[:, at] = split(mm(t, rh[at, :], NT) + mm(t, rl[at, :], NT))
        for a in tiles:
            x = t_ref[c * CH:(c + 1) * CH, a].astype(jnp.float32)
            if depth:
                x = x - (mm(sh[:, :depth], rh[:depth, a]) + (mm(sl[:, :depth], rh[:depth, a]) + mm(sh[:, :depth], rl[:depth, a])))
            v[slot, :, a] = x
            vh[slot, :, a], vl[slot, :, a] = split(x)

    def products(c, d):
        a, b = c % 2, d % 2
        low = mm(vh[a], vl[b], NT)
        other = low.T if c == d else mm(vl[a], vh[b], NT)
        return mm(vh[a], vh[b], NT) + (low + other)

    def finish(c, x):
        slot = c % 2
        xh, xl = split(x)
        at = slice(prev + c * CH, prev + (c + 1) * CH)
        for a in tiles:
            q = mm(xh, vh[slot, :, a]) + (mm(xl, vh[slot, :, a]) + mm(xh, vl[slot, :, a]))
            rh[at, a], rl[at, a] = split(q)

    def correct(c, s):
        slot = c % 2
        th, tl = split(s.T)
        at = slice(prev + (c - 1) * CH, prev + c * CH)
        for a in tiles:
            x = v[slot, :, a] - (mm(th, rh[at, a]) + (mm(tl, rh[at, a]) + mm(th, rl[at, a])))
            v[slot, :, a] = x
            vh[slot, :, a], vl[slot, :, a] = split(x)

    remove(0, prev)
    g = products(0, 0)
    x = s = None
    for c in range(chunks):
        if c:
            finish(c - 1, x)
            correct(c, s)
        if c + 1 < chunks:
            remove(c + 1, prev + c * CH)
            cross = products(c, c + 1)
            ahead = products(c + 1, c + 1)
        x = inverse_of_chunk(g)
        if c + 1 < chunks:
            s = mm3(x, cross)
            g = ahead - mm3(s.T, s)
    finish(chunks - 1, x)
    if prev:
        part = own.shape[1]
        at = pl.ds(pl.multiple_of(lax.axis_index("fsdp") * part, part), part)
        own[...] = rh[:, at].astype(jnp.float32) + rl[:, at].astype(jnp.float32)

def orthogonal_rows(t, done=None):
    count, width = t.shape
    prev = 0 if done is None else done[0].shape[0]
    shape = jax.ShapeDtypeStruct((prev + count, width), jnp.bfloat16)
    args = (t,) if done is None else (t,) + tuple(done)
    n = prev + count
    scratch = [pltpu.VMEM((2, CH, width), jnp.float32)] + [pltpu.VMEM((2, CH, width), jnp.bfloat16)] * 2
    scratch += [pltpu.VMEM((CH, n), jnp.bfloat16)] * 2
    outs = (shape, shape)
    if prev:
        scratch += [pltpu.VMEM((n, width), jnp.bfloat16)]
        outs = (shape, jax.ShapeDtypeStruct((n, width // lax.axis_size("fsdp")), jnp.float32))
    return pl.pallas_call(
        functools.partial(kernel, prev, count),
        out_shape=outs,
        scratch_shapes=scratch,
        compiler_params=pltpu.CompilerParams(vmem_limit_bytes=56 * 1024 * 1024),
    )(*args)


def rotate_kernel(q_ref, gradient_ref, moment_ref, second_ref, two_ref, raw_ref, square_ref):
    step = pl.program_id(0)
    q = q_ref[...]
    order = q.shape[1]
    width = gradient_ref.shape[1]

    @pl.when(step == 0)
    def _():
        raw_ref[...] = jnp.zeros_like(raw_ref)

    for a in range(0, width, CH):
        at = slice(a, a + CH)
        grad_rot = mm(q, gradient_ref[:, at])
        moment_rot = mm(q, moment_ref[:, at])
        two = beta_two * second_ref[:, at] + (1.0 - beta_two) * jnp.square(grad_rot)
        two_ref[:, at] = two
        ratio = (moment_rot / (jnp.sqrt(two) + small_eps)).T.astype(jnp.bfloat16)
        for o in range(0, order, CH):
            raw_ref[at, o:o + CH] += mm(ratio, q_ref[:, o:o + CH])

    @pl.when(step == pl.num_programs(0) - 1)
    def _():
        square_ref[...] = jnp.sum(jnp.square(raw_ref[...]), axis=0, keepdims=True)


def rotate(basis, gradient, moment_half, second_in):
    rows, order = basis.shape
    width = gradient.shape[1]
    whole = pl.BlockSpec((order, width), lambda i: (0, 0))
    band = pl.BlockSpec((BAND, width), lambda i: (i, 0))
    return pl.pallas_call(
        rotate_kernel,
        grid=(rows // BAND,),
        in_specs=[pl.BlockSpec((BAND, order), lambda i: (i, 0)), whole, whole, band],
        out_specs=(band, pl.BlockSpec((width, order), lambda i: (0, 0)), pl.BlockSpec((1, order), lambda i: (0, 0))),
        out_shape=(
            jax.ShapeDtypeStruct((rows, width), jnp.float32),
            jax.ShapeDtypeStruct((width, order), jnp.float32),
            jax.ShapeDtypeStruct((1, order), jnp.float32),
        ),
        compiler_params=pltpu.CompilerParams(vmem_limit_bytes=48 * 1024 * 1024),
    )(basis, gradient, moment_half, second_in)


def sum_over_all(x):
    axes = ("owner", "fsdp")
    size = lax.axis_size(axes)
    copies = jnp.broadcast_to(x, (size, 128))
    return jnp.sum(lax.all_to_all(copies, axes, 0, 0, tiled=True)[:, :1], axis=0, keepdims=True)


def on_device(precond, basis_old, gradient, moment_in, second_in):
    order = precond.shape[2]
    width = gradient.shape[1]
    both = jnp.concatenate([precond[0], basis_old[0, :, :FIRST]], axis=1)
    both = lax.all_gather(both, "fsdp", axis=0, tiled=True)
    factor = both[:, :order]
    later = lax.all_gather(basis_old[0, :, FIRST:], "fsdp", axis=0, tiled=True)
    moment_one = beta_one * moment_in + (1.0 - beta_one) * gradient.astype(jnp.float32)
    moment_half = moment_one.astype(jnp.bfloat16)
    first_rows = mm(both[:, order:], factor, TN).astype(jnp.bfloat16)
    first = orthogonal_rows(first_rows)
    later_rows = mm(later, factor, TN).astype(jnp.bfloat16)
    high, own = orthogonal_rows(later_rows, first)
    basis_new = own.T[None]
    moment_two, turned, squares = rotate(high, gradient, moment_half, second_in)
    unscaled_update = lax.optimization_barrier(turned.T)
    total = sum_over_all(jnp.sum(squares).reshape(1, 1))
    count = gradient.shape[0] * lax.axis_size("owner") * width * lax.axis_size("fsdp")
    scale = jnp.sqrt(jnp.float32(count)) / (jnp.sqrt(total) + norm_eps)
    update = (unscaled_update * scale).astype(jnp.bfloat16)
    return (update, moment_one, moment_two, basis_new)


def solution(mesh):
    return jax.shard_map(
        on_device,
        mesh=mesh,
        in_specs=(
            P("owner", "fsdp", None),
            P("owner", "fsdp", None),
            P("owner", "fsdp"),
            P("owner", "fsdp"),
            P("owner", "fsdp"),
        ),
        out_specs=(
            P("owner", "fsdp"),
            P("owner", "fsdp"),
            P("owner", "fsdp"),
            P("owner", "fsdp", None),
        ),
        check_vma=False,
    )
```

```python
import functools
import jax
import jax.numpy as jnp
from jax import lax
from jax.experimental import pallas as pl
from jax.experimental.pallas import tpu as pltpu
from jax.sharding import PartitionSpec as P

beta_one = 0.9
beta_two = 0.95
small_eps = 1e-08
norm_eps = 1e-06
NN = (((1,), (0,)), ((), ()))
NT = (((1,), (1,)), ((), ()))
TN = (((0,), (0,)), ((), ()))
CH = 256
FIRST = 1024
BAND = 512

def lane_splat(row, lane):
    return jnp.broadcast_to(row[:, lane:lane+1], (8, 128))

def diag_pick(row, start):
    idx = lax.broadcasted_iota(jnp.int32, (8, 128), 0) + start
    return jnp.take_along_axis(row, idx, axis=1, mode="promise_in_bounds")

def invert_factor(A):
    sub = lax.broadcasted_iota(jnp.int32, (8, 128), 0)
    lane = lax.broadcasted_iota(jnp.int32, (8, 128), 1)
    A = list(A)
    X = [(lane == sub + 8 * g).astype(jnp.float32) for g in range(16)]
    for g in range(16):
        r = [jnp.broadcast_to(A[g][k:k+1, :], (8, 128)) for k in range(8)]
        x = [jnp.broadcast_to(X[g][k:k+1, :], (8, 128)) for k in range(8)]
        d = {}
        for j in range(8):
            for i in range(j, 8):
                d[i, j] = lane_splat(r[j], 8 * g + i)
        for k in range(8):
            rs = lax.rsqrt(d[k, k])
            rd = rs * rs
            for i in range(k + 1, 8):
                m = d[i, k] * rd
                for j in range(k + 1, i + 1):
                    d[i, j] = d[i, j] - m * d[j, k]
                r[i] = r[i] - m * r[k]
                x[i] = x[i] - m * x[k]
            r[k] = r[k] * rs
            x[k] = x[k] * rs
        for h in range(g + 1, 16):
            for k in range(8):
                l = diag_pick(r[k], 8 * h)
                A[h] = A[h] - l * r[k]
                X[h] = X[h] - l * x[k]
        z = x[0]
        for k in range(1, 8):
            z = jnp.where(sub == k, x[k], z)
        X[g] = z
    return X


def mm(a, b, dims=NN):
    return lax.dot_general(a, b, dims, preferred_element_type=jnp.float32)

def split(x):
    high = x.astype(jnp.bfloat16)
    return high, (x - high.astype(jnp.float32)).astype(jnp.bfloat16)

def mm3(a, b, dims=NN):
    ah, al = split(a)
    bh, bl = split(b)
    return mm(ah, bh, dims) + (mm(al, bh, dims) + mm(ah, bl, dims))

def inverse_of_rows(block):
    rows = invert_factor([block[8 * i:8 * i + 8, :] for i in range(16)])
    return jnp.concatenate(rows, axis=0)

def inverse_of_chunk(g):
    h = CH // 2
    x1 = inverse_of_rows(g[:h, :h])
    u = mm3(x1, g[:h, h:])
    ut = u.T
    w = mm3(ut, x1)
    x2 = inverse_of_rows(g[h:, h:] - mm3(ut, u))
    x21 = -mm3(x2, w)
    top = jnp.concatenate([x1, jnp.zeros((h, h), jnp.float32)], axis=1)
    return jnp.concatenate([top, jnp.concatenate([x21, x2], axis=1)], axis=0)

def kernel(prev, count, *refs):
    if prev:
        t_ref, ph_ref, pl_ref, rh, own, v, vh, vl, sh, sl, rl = refs
        rh[0:prev, :] = ph_ref[...]
        rl[0:prev, :] = pl_ref[...]
    else:
        t_ref, rh, rl, v, vh, vl, sh, sl = refs
    width = t_ref.shape[1]
    tiles = [slice(a, a + CH) for a in range(0, width, CH)]
    chunks = count // CH

    def remove(c, depth):
        slot = c % 2
        t = t_ref[c * CH:(c + 1) * CH, :]
        for p in range(0, depth, CH):
            at = slice(p, p + CH)
            sh[:, at], sl[:, at] = split(mm(t, rh[at, :], NT) + mm(t, rl[at, :], NT))
        for a in tiles:
            x = t_ref[c * CH:(c + 1) * CH, a].astype(jnp.float32)
            if depth:
                x = x - (mm(sh[:, :depth], rh[:depth, a]) + (mm(sl[:, :depth], rh[:depth, a]) + mm(sh[:, :depth], rl[:depth, a])))
            v[slot, :, a] = x
            vh[slot, :, a], vl[slot, :, a] = split(x)

    def products(c, d):
        a, b = c % 2, d % 2
        low = mm(vh[a], vl[b], NT)
        other = low.T if c == d else mm(vl[a], vh[b], NT)
        return mm(vh[a], vh[b], NT) + (low + other)

    def finish(c, x):
        slot = c % 2
        xh, xl = split(x)
        at = slice(prev + c * CH, prev + (c + 1) * CH)
        for a in tiles:
            q = mm(xh, vh[slot, :, a]) + (mm(xl, vh[slot, :, a]) + mm(xh, vl[slot, :, a]))
            rh[at, a], rl[at, a] = split(q)

    def correct(c, s):
        slot = c % 2
        th, tl = split(s.T)
        at = slice(prev + (c - 1) * CH, prev + c * CH)
        for a in tiles:
            x = v[slot, :, a] - (mm(th, rh[at, a]) + (mm(tl, rh[at, a]) + mm(th, rl[at, a])))
            v[slot, :, a] = x
            vh[slot, :, a], vl[slot, :, a] = split(x)

    remove(0, prev)
    g = products(0, 0)
    x = s = None
    for c in range(chunks):
        if c:
            finish(c - 1, x)
            correct(c, s)
        if c + 1 < chunks:
            remove(c + 1, prev + c * CH)
            cross = products(c, c + 1)
            ahead = products(c + 1, c + 1)
        x = inverse_of_chunk(g)
        if c + 1 < chunks:
            s = mm3(x, cross)
            g = ahead - mm3(s.T, s)
    finish(chunks - 1, x)
    if prev:
        part = own.shape[1]
        at = pl.ds(pl.multiple_of(lax.axis_index("fsdp") * part, part), part)
        own[...] = rh[:, at].astype(jnp.float32) + rl[:, at].astype(jnp.float32)

def orthogonal_rows(t, done=None):
    count, width = t.shape
    prev = 0 if done is None else done[0].shape[0]
    shape = jax.ShapeDtypeStruct((prev + count, width), jnp.bfloat16)
    args = (t,) if done is None else (t,) + tuple(done)
    n = prev + count
    scratch = [pltpu.VMEM((2, CH, width), jnp.float32)] + [pltpu.VMEM((2, CH, width), jnp.bfloat16)] * 2
    scratch += [pltpu.VMEM((CH, n), jnp.bfloat16)] * 2
    outs = (shape, shape)
    if prev:
        scratch += [pltpu.VMEM((n, width), jnp.bfloat16)]
        outs = (shape, jax.ShapeDtypeStruct((n, width // lax.axis_size("fsdp")), jnp.float32))
    return pl.pallas_call(
        functools.partial(kernel, prev, count),
        out_shape=outs,
        scratch_shapes=scratch,
        compiler_params=pltpu.CompilerParams(vmem_limit_bytes=56 * 1024 * 1024),
    )(*args)


def pack_kernel(count, precond_ref, basis_ref, sent_ref, later_ref):
    part = precond_ref.shape[0]
    me = lax.axis_index("fsdp")
    span = count // 2 + 1
    for s in range(span):
        at = pl.multiple_of(lax.rem(me + s, count) * part, part)
        sent_ref[:, s * part:(s + 1) * part] = precond_ref[:, pl.ds(at, part)]
    sent_ref[:, span * part:] = basis_ref[:, :FIRST]
    later_ref[...] = basis_ref[:, FIRST:]


def pack(precond, basis):
    part, order = precond.shape
    count = order // part
    return pl.pallas_call(
        functools.partial(pack_kernel, count),
        out_shape=(
            jax.ShapeDtypeStruct((part, (count // 2 + 1) * part + FIRST), precond.dtype),
            jax.ShapeDtypeStruct((part, order - FIRST), basis.dtype),
        ),
    )(precond, basis)


def power_kernel(part, both_ref, factor_ref, rows_ref):
    order = factor_ref.shape[0]
    count = order // part
    span = count // 2 + 1
    for k in range(count):
        here = slice(k * part, (k + 1) * part)
        for s in range(span):
            there = slice((k + s) % count * part, ((k + s) % count + 1) * part)
            block = both_ref[here, s * part:(s + 1) * part]
            factor_ref[here, there] = block
            if 0 < s < span - 1:
                factor_ref[there, here] = block.T
    for a in range(0, FIRST, CH):
        columns = both_ref[:, span * part + a:span * part + a + CH].T
        for o in range(0, order, CH):
            rows_ref[a:a + CH, o:o + CH] = mm(columns, factor_ref[:, o:o + CH]).astype(jnp.bfloat16)


def power(both, part):
    order = both.shape[0]
    return pl.pallas_call(
        functools.partial(power_kernel, part),
        out_shape=(
            jax.ShapeDtypeStruct((order, order), both.dtype),
            jax.ShapeDtypeStruct((FIRST, order), both.dtype),
        ),
        compiler_params=pltpu.CompilerParams(vmem_limit_bytes=48 * 1024 * 1024),
    )(both)


def rotate_kernel(q_ref, gradient_ref, moment_ref, second_ref, two_ref, raw_ref, square_ref):
    step = pl.program_id(0)
    q = q_ref[...]
    order = q.shape[1]
    width = gradient_ref.shape[1]

    @pl.when(step == 0)
    def _():
        raw_ref[...] = jnp.zeros_like(raw_ref)

    for a in range(0, width, CH):
        at = slice(a, a + CH)
        grad_rot = mm(q, gradient_ref[:, at])
        moment_rot = mm(q, moment_ref[:, at])
        two = beta_two * second_ref[:, at] + (1.0 - beta_two) * jnp.square(grad_rot)
        two_ref[:, at] = two
        ratio = (moment_rot / (jnp.sqrt(two) + small_eps)).T.astype(jnp.bfloat16)
        for o in range(0, order, CH):
            raw_ref[at, o:o + CH] += mm(ratio, q_ref[:, o:o + CH])

    @pl.when(step == pl.num_programs(0) - 1)
    def _():
        square_ref[...] = jnp.sum(jnp.square(raw_ref[...]), axis=0, keepdims=True)


def rotate(basis, gradient, moment_half, second_in):
    rows, order = basis.shape
    width = gradient.shape[1]
    whole = pl.BlockSpec((order, width), lambda i: (0, 0))
    band = pl.BlockSpec((BAND, width), lambda i: (i, 0))
    return pl.pallas_call(
        rotate_kernel,
        grid=(rows // BAND,),
        in_specs=[pl.BlockSpec((BAND, order), lambda i: (i, 0)), whole, whole, band],
        out_specs=(band, pl.BlockSpec((width, order), lambda i: (0, 0)), pl.BlockSpec((1, order), lambda i: (0, 0))),
        out_shape=(
            jax.ShapeDtypeStruct((rows, width), jnp.float32),
            jax.ShapeDtypeStruct((width, order), jnp.float32),
            jax.ShapeDtypeStruct((1, order), jnp.float32),
        ),
        compiler_params=pltpu.CompilerParams(vmem_limit_bytes=48 * 1024 * 1024),
    )(basis, gradient, moment_half, second_in)


def sum_over_all(x):
    axes = ("owner", "fsdp")
    size = lax.axis_size(axes)
    copies = jnp.broadcast_to(x, (size, 128))
    return jnp.sum(lax.all_to_all(copies, axes, 0, 0, tiled=True)[:, :1], axis=0, keepdims=True)


def on_device(precond, basis_old, gradient, moment_in, second_in):
    width = gradient.shape[1]
    sent, later = pack(precond[0], basis_old[0])
    both = lax.all_gather(sent, "fsdp", axis=0, tiled=True)
    later = lax.all_gather(later, "fsdp", axis=0, tiled=True)
    moment_one = beta_one * moment_in + (1.0 - beta_one) * gradient.astype(jnp.float32)
    moment_half = moment_one.astype(jnp.bfloat16)
    factor, first_rows = power(both, precond.shape[1])
    first = orthogonal_rows(first_rows)
    later_rows = mm(later, factor, TN).astype(jnp.bfloat16)
    high, own = orthogonal_rows(later_rows, first)
    basis_new = own.T[None]
    moment_two, turned, squares = rotate(high, gradient, moment_half, second_in)
    total = sum_over_all(jnp.sum(squares).reshape(1, 1))
    count = gradient.shape[0] * lax.axis_size("owner") * width * lax.axis_size("fsdp")
    scale = jnp.sqrt(jnp.float32(count)) / (jnp.sqrt(total) + norm_eps)
    update = (turned.T * scale).astype(jnp.bfloat16)
    return (update, moment_one, moment_two, basis_new)


def solution(mesh):
    return jax.shard_map(
        on_device,
        mesh=mesh,
        in_specs=(
            P("owner", "fsdp", None),
            P("owner", "fsdp", None),
            P("owner", "fsdp"),
            P("owner", "fsdp"),
            P("owner", "fsdp"),
        ),
        out_specs=(
            P("owner", "fsdp"),
            P("owner", "fsdp"),
            P("owner", "fsdp"),
            P("owner", "fsdp", None),
        ),
        check_vma=False,
    )
```

```python
import functools
import jax
import jax.numpy as jnp
from jax import lax
from jax.experimental import pallas as pl
from jax.experimental.pallas import tpu as pltpu
from jax.sharding import PartitionSpec as P

beta_one = 0.9
beta_two = 0.95
small_eps = 1e-08
norm_eps = 1e-06
NN = (((1,), (0,)), ((), ()))
NT = (((1,), (1,)), ((), ()))
TN = (((0,), (0,)), ((), ()))
CH = 256
FIRST = 1024
BAND = 512

def lane_splat(row, lane):
    return jnp.broadcast_to(row[:, lane:lane+1], (8, 128))

def diag_pick(row, start):
    idx = lax.broadcasted_iota(jnp.int32, (8, 128), 0) + start
    return jnp.take_along_axis(row, idx, axis=1, mode="promise_in_bounds")

def invert_factor(A):
    sub = lax.broadcasted_iota(jnp.int32, (8, 128), 0)
    lane = lax.broadcasted_iota(jnp.int32, (8, 128), 1)
    A = list(A)
    X = [(lane == sub + 8 * g).astype(jnp.float32) for g in range(16)]
    for g in range(16):
        r = [jnp.broadcast_to(A[g][k:k+1, :], (8, 128)) for k in range(8)]
        x = [jnp.broadcast_to(X[g][k:k+1, :], (8, 128)) for k in range(8)]
        d = {}
        for j in range(8):
            for i in range(j, 8):
                d[i, j] = lane_splat(r[j], 8 * g + i)
        for k in range(8):
            rs = lax.rsqrt(d[k, k])
            rd = rs * rs
            for i in range(k + 1, 8):
                m = d[i, k] * rd
                for j in range(k + 1, i + 1):
                    d[i, j] = d[i, j] - m * d[j, k]
                r[i] = r[i] - m * r[k]
                x[i] = x[i] - m * x[k]
            r[k] = r[k] * rs
            x[k] = x[k] * rs
        for h in range(g + 1, 16):
            for k in range(8):
                l = diag_pick(r[k], 8 * h)
                A[h] = A[h] - l * r[k]
                X[h] = X[h] - l * x[k]
        z = x[0]
        for k in range(1, 8):
            z = jnp.where(sub == k, x[k], z)
        X[g] = z
    return X


def mm(a, b, dims=NN):
    return lax.dot_general(a, b, dims, preferred_element_type=jnp.float32)

def split(x):
    high = x.astype(jnp.bfloat16)
    return high, (x - high.astype(jnp.float32)).astype(jnp.bfloat16)

def left(x):
    high, low = split(x)
    return jnp.concatenate([high, low, high], axis=1)

def right(high, low):
    return jnp.concatenate([high, high, low], axis=0)

def mm3(a, b):
    return mm(left(a), right(*split(b)))

def inverse_of_rows(block):
    rows = invert_factor([block[8 * i:8 * i + 8, :] for i in range(16)])
    return jnp.concatenate(rows, axis=0)

def inverse_of_chunk(g):
    h = CH // 2
    x1 = inverse_of_rows(g[:h, :h])
    u = mm3(x1, g[:h, h:])
    ut = u.T
    w = mm3(ut, x1)
    x2 = inverse_of_rows(g[h:, h:] - mm3(ut, u))
    x21 = -mm3(x2, w)
    top = jnp.concatenate([x1, jnp.zeros((h, h), jnp.float32)], axis=1)
    return jnp.concatenate([top, jnp.concatenate([x21, x2], axis=1)], axis=0)

def kernel(prev, count, *refs):
    if prev:
        t_ref, ph_ref, pl_ref, rh, own, v, vh, vl, sh, sl, rl = refs
        rh[0:prev, :] = ph_ref[...]
        rl[0:prev, :] = pl_ref[...]
    else:
        t_ref, rh, rl, v, vh, vl, sh, sl = refs
    width = t_ref.shape[1]
    tiles = [slice(a, a + CH) for a in range(0, width, CH)]
    chunks = count // CH

    def remove(c, depth):
        slot = c % 2
        t = t_ref[c * CH:(c + 1) * CH, :]
        for p in range(0, depth, CH):
            at = slice(p, p + CH)
            sh[:, at], sl[:, at] = split(mm(t, rh[at, :], NT) + mm(t, rl[at, :], NT))
        for a in tiles:
            x = t_ref[c * CH:(c + 1) * CH, a].astype(jnp.float32)
            if depth:
                x = x - (mm(sh[:, :depth], rh[:depth, a]) + (mm(sl[:, :depth], rh[:depth, a]) + mm(sh[:, :depth], rl[:depth, a])))
            v[slot, :, a] = x
            vh[slot, :, a], vl[slot, :, a] = split(x)

    def products(c, d):
        a, b = c % 2, d % 2
        low = mm(vh[a], vl[b], NT)
        other = low.T if c == d else mm(vl[a], vh[b], NT)
        return mm(vh[a], vh[b], NT) + (low + other)

    def finish(c, x):
        slot = c % 2
        x3 = left(x)
        at = slice(prev + c * CH, prev + (c + 1) * CH)
        for a in tiles:
            q = mm(x3, right(vh[slot, :, a], vl[slot, :, a]))
            rh[at, a], rl[at, a] = split(q)

    def correct(c, s):
        slot = c % 2
        t3 = left(s.T)
        at = slice(prev + (c - 1) * CH, prev + c * CH)
        for a in tiles:
            x = v[slot, :, a] - mm(t3, right(rh[at, a], rl[at, a]))
            v[slot, :, a] = x
            vh[slot, :, a], vl[slot, :, a] = split(x)

    remove(0, prev)
    g = products(0, 0)
    x = s = None
    for c in range(chunks):
        if c:
            finish(c - 1, x)
            correct(c, s)
        if c + 1 < chunks:
            remove(c + 1, prev + c * CH)
            cross = products(c, c + 1)
            ahead = products(c + 1, c + 1)
        x = inverse_of_chunk(g)
        if c + 1 < chunks:
            s = mm3(x, cross)
            g = ahead - mm3(s.T, s)
    finish(chunks - 1, x)
    if prev:
        part = own.shape[1]
        at = pl.ds(pl.multiple_of(lax.axis_index("fsdp") * part, part), part)
        own[...] = rh[:, at].astype(jnp.float32) + rl[:, at].astype(jnp.float32)

def orthogonal_rows(t, done=None):
    count, width = t.shape
    prev = 0 if done is None else done[0].shape[0]
    shape = jax.ShapeDtypeStruct((prev + count, width), jnp.bfloat16)
    args = (t,) if done is None else (t,) + tuple(done)
    n = prev + count
    scratch = [pltpu.VMEM((2, CH, width), jnp.float32)] + [pltpu.VMEM((2, CH, width), jnp.bfloat16)] * 2
    scratch += [pltpu.VMEM((CH, n), jnp.bfloat16)] * 2
    outs = (shape, shape)
    if prev:
        scratch += [pltpu.VMEM((n, width), jnp.bfloat16)]
        outs = (shape, jax.ShapeDtypeStruct((n, width // lax.axis_size("fsdp")), jnp.float32))
    return pl.pallas_call(
        functools.partial(kernel, prev, count),
        out_shape=outs,
        scratch_shapes=scratch,
        compiler_params=pltpu.CompilerParams(vmem_limit_bytes=56 * 1024 * 1024),
    )(*args)


def pack_kernel(count, precond_ref, basis_ref, sent_ref, later_ref):
    part = precond_ref.shape[0]
    me = lax.axis_index("fsdp")
    span = count // 2 + 1
    for s in range(span):
        at = pl.multiple_of(lax.rem(me + s, count) * part, part)
        sent_ref[:, s * part:(s + 1) * part] = precond_ref[:, pl.ds(at, part)]
    sent_ref[:, span * part:] = basis_ref[:, :FIRST]
    later_ref[...] = basis_ref[:, FIRST:]


def pack(precond, basis):
    part, order = precond.shape
    count = order // part
    return pl.pallas_call(
        functools.partial(pack_kernel, count),
        out_shape=(
            jax.ShapeDtypeStruct((part, (count // 2 + 1) * part + FIRST), precond.dtype),
            jax.ShapeDtypeStruct((part, order - FIRST), basis.dtype),
        ),
    )(precond, basis)


def power_kernel(part, both_ref, factor_ref, rows_ref):
    order = factor_ref.shape[0]
    count = order // part
    span = count // 2 + 1
    for k in range(count):
        here = slice(k * part, (k + 1) * part)
        for s in range(span):
            there = slice((k + s) % count * part, ((k + s) % count + 1) * part)
            block = both_ref[here, s * part:(s + 1) * part]
            factor_ref[here, there] = block
            if 0 < s < span - 1:
                factor_ref[there, here] = block.T
    for a in range(0, FIRST, CH):
        columns = both_ref[:, span * part + a:span * part + a + CH].T
        for o in range(0, order, CH):
            rows_ref[a:a + CH, o:o + CH] = mm(columns, factor_ref[:, o:o + CH]).astype(jnp.bfloat16)


def power(both, part):
    order = both.shape[0]
    return pl.pallas_call(
        functools.partial(power_kernel, part),
        out_shape=(
            jax.ShapeDtypeStruct((order, order), both.dtype),
            jax.ShapeDtypeStruct((FIRST, order), both.dtype),
        ),
        compiler_params=pltpu.CompilerParams(vmem_limit_bytes=48 * 1024 * 1024),
    )(both)


def rotate_kernel(q_ref, gradient_ref, moment_ref, second_ref, two_ref, raw_ref, square_ref):
    step = pl.program_id(0)
    q = q_ref[...]
    order = q.shape[1]
    width = gradient_ref.shape[1]

    @pl.when(step == 0)
    def _():
        raw_ref[...] = jnp.zeros_like(raw_ref)

    for a in range(0, width, CH):
        at = slice(a, a + CH)
        grad_rot = mm(q, gradient_ref[:, at])
        moment_rot = mm(q, moment_ref[:, at])
        two = beta_two * second_ref[:, at] + (1.0 - beta_two) * jnp.square(grad_rot)
        two_ref[:, at] = two
        ratio = (moment_rot / (jnp.sqrt(two) + small_eps)).T.astype(jnp.bfloat16)
        for o in range(0, order, CH):
            raw_ref[at, o:o + CH] += mm(ratio, q_ref[:, o:o + CH])

    @pl.when(step == pl.num_programs(0) - 1)
    def _():
        columns = jnp.sum(jnp.square(raw_ref[...]), axis=0, keepdims=True)
        square_ref[...] = jnp.broadcast_to(jnp.sum(columns, axis=1, keepdims=True), square_ref.shape)


def rotate(basis, gradient, moment_half, second_in, copies):
    rows, order = basis.shape
    width = gradient.shape[1]
    whole = pl.BlockSpec((order, width), lambda i: (0, 0))
    band = pl.BlockSpec((BAND, width), lambda i: (i, 0))
    return pl.pallas_call(
        rotate_kernel,
        grid=(rows // BAND,),
        in_specs=[pl.BlockSpec((BAND, order), lambda i: (i, 0)), whole, whole, band],
        out_specs=(band, pl.BlockSpec((width, order), lambda i: (0, 0)), pl.BlockSpec((copies, 128), lambda i: (0, 0))),
        out_shape=(
            jax.ShapeDtypeStruct((rows, width), jnp.float32),
            jax.ShapeDtypeStruct((width, order), jnp.float32),
            jax.ShapeDtypeStruct((copies, 128), jnp.float32),
        ),
        compiler_params=pltpu.CompilerParams(vmem_limit_bytes=48 * 1024 * 1024),
    )(basis, gradient, moment_half, second_in)


def sum_over_all(copies):
    axes = ("owner", "fsdp")
    return jnp.sum(lax.all_to_all(copies, axes, 0, 0, tiled=True)[:, :1], axis=0, keepdims=True)


def on_device(precond, basis_old, gradient, moment_in, second_in):
    width = gradient.shape[1]
    sent, later = pack(precond[0], basis_old[0])
    both = lax.all_gather(sent, "fsdp", axis=0, tiled=True)
    later = lax.all_gather(later, "fsdp", axis=0, tiled=True)
    moment_one = beta_one * moment_in + (1.0 - beta_one) * gradient.astype(jnp.float32)
    moment_half = moment_one.astype(jnp.bfloat16)
    factor, first_rows = power(both, precond.shape[1])
    first = orthogonal_rows(first_rows)
    later_rows = mm(later, factor, TN).astype(jnp.bfloat16)
    high, own = orthogonal_rows(later_rows, first)
    basis_new = own.T[None]
    moment_two, turned, squares = rotate(
        high, gradient, moment_half, second_in, lax.axis_size(("owner", "fsdp"))
    )
    total = sum_over_all(squares)
    count = gradient.shape[0] * lax.axis_size("owner") * width * lax.axis_size("fsdp")
    scale = jnp.sqrt(jnp.float32(count)) / (jnp.sqrt(total) + norm_eps)
    update = (turned.T * scale).astype(jnp.bfloat16)
    return (update, moment_one, moment_two, basis_new)


def solution(mesh):
    return jax.shard_map(
        on_device,
        mesh=mesh,
        in_specs=(
            P("owner", "fsdp", None),
            P("owner", "fsdp", None),
            P("owner", "fsdp"),
            P("owner", "fsdp"),
            P("owner", "fsdp"),
        ),
        out_specs=(
            P("owner", "fsdp"),
            P("owner", "fsdp"),
            P("owner", "fsdp"),
            P("owner", "fsdp", None),
        ),
        check_vma=False,
    )
```
